32 devices in a mesh: dp: 8 (over z, y), tensor: 4 (over x, core).
Axes of the slice: x: 2, y: 2, z: 4, core: 2. Of those that a mesh axis runs over, the one named last changes fastest.
Arguments:
- cotangent: bfloat16 [1024, 8192], P('dp'), may hold values from -6 to 6
- inputs: bfloat16 [1024, 8192], P('dp'), may hold values from -6 to 6
- gate_saved: bfloat16 [1024, 14336], P('dp', 'tensor'), may hold values from -6 to 6
- up_saved: bfloat16 [1024, 14336], P('dp', 'tensor'), may hold values from -6 to 6
- gate_weight: bfloat16 [8192, 14336], P('dp', 'tensor'), may hold values from -0.09375 to 0.09375
- up_weight: bfloat16 [8192, 14336], P('dp', 'tensor'), may hold values from -0.0625 to 0.0625
- down_weight: bfloat16 [8192, 14336], P('dp', 'tensor'), may hold values from -0.046875 to 0.046875
- scale_table: float32 [16], replicated, may hold values from 0.5 to 2
- scale_index: int32 [14336], P('tensor'), may hold values from 0 to 15
- clip_mask: int32 [14336], P('tensor'), may hold values 0 or 1
Outputs:
- input_grad: bfloat16 [1024, 8192], P('dp', 'tensor')
- rotation_grad: float32 [8192, 8192], P('dp', 'tensor')
The draws below stay inside these ranges and needn't reach their ends.
All inputs are finite; a program needn't handle non-finite values. No bound on the sum of `clip_mask` on one device may be relied on, other than what follows from the above.
Results may differ from the reference program's by a relative error of at most 0.012.
Values may be sent and summed in bfloat16 or wider, within the bound.
A program may use at most 384 MiB of HBM per device.

```python
import math
import jax
import jax.numpy as jnp
from jax import lax

D = 8192
FF = 14336
HB = 128
LEVELS = 16
TOKENS = 1024
N_TENSOR = 4


def set_ends(result, key, low, largest):
    dims = result.shape
    index_at = [jax.random.randint(jax.random.fold_in(key, axis), (), 0, dims[axis]) for axis in range(len(dims))]
    result = result.at[tuple(index_at)].set(low)
    longest = dims.index(max(dims))
    index_at[longest] = (index_at[longest] + 1) % dims[longest]
    return result.at[tuple(index_at)].set(largest)


def with_spikes(values, stream_key, source, target, shards_of, factor):
    def block_of(dim):
        return (jnp.arange(values.shape[dim]) // (values.shape[dim] // shards_of)).reshape((-1,) + (1,) * (values.ndim - 1 - dim))

    one_side = jax.random.permutation(stream_key, shards_of)[block_of(target)]
    second = (block_of(target) + shards_of // 2) % shards_of
    return jnp.where((block_of(source) == one_side) | (block_of(source) == second), factor * values, values)


def block_levels(rng, shape, split, smallest, top_value):
    level = 1.0
    for dim, shards_of in split:
        draws = jax.random.uniform(jax.random.fold_in(jax.random.fold_in(rng, 6), dim), (shards_of,), jnp.float32, smallest / len(split), top_value / len(split))
        level = level * jnp.repeat(jnp.exp(draws), shape[dim] // shards_of).reshape((-1,) + (1,) * (len(shape) - 1 - dim))
    return level


def gaussian(key, shape, spread, most, shards=(), held_as=jnp.bfloat16):
    level = block_levels(key, shape, shards, -0.22, 0.18) if shards else 1.0
    entries = jax.random.normal(key, shape, jnp.float32) * spread * level
    return jnp.minimum(jnp.maximum(entries, -most), most).astype(held_as)


def heavy_noise(rng, extent, width, most, split, heavy, kind=jnp.bfloat16):
    drawn = width * jax.random.normal(rng, extent, jnp.float32)
    if split:
        drawn = drawn * block_levels(rng, extent, split, -0.22, 0.18)
    return jnp.clip(with_spikes(drawn, jax.random.fold_in(rng, 3), *heavy), -most, most).astype(kind)


def setup_inputs(seed: int = 0) -> dict:
    keys = jax.random.split(jax.random.key(seed), 11)
    cotangent = gaussian(keys[0], (TOKENS, D), 1.0, 6.0, ((0, 8),))
    inputs = heavy_noise(keys[1], (TOKENS, D), 1.0, 6.0, ((0, 8),), (0, 1, 8, 2.0))
    gate_saved = gaussian(keys[2], (TOKENS, FF), 1.0, 6.0, ((0, 8), (1, 4)))
    up_saved = gaussian(keys[3], (TOKENS, FF), 1.0, 6.0, ((0, 8), (1, 4)))
    gate_weight = heavy_noise(keys[4], (D, FF), D ** -0.5, 0.09375, ((0, 8), (1, 4)), (1, 0, 8, 2.0))
    up_weight = gaussian(keys[5], (D, FF), D ** -0.5, 0.0625, ((0, 8), (1, 4)))
    down_weight = gaussian(keys[6], (D, FF), FF ** -0.5, 0.046875, ((0, 8), (1, 4)))
    scale_table = jnp.clip(jnp.exp(jax.random.uniform(keys[7], (LEVELS,), jnp.float32, math.log(0.5), math.log(2.0))), 0.5, 2.0)
    scale_index = set_ends(jax.random.randint(keys[8], (FF,), 0, LEVELS), jax.random.fold_in(keys[8], 1), 0, LEVELS - 1).astype(jnp.int32)
    clip_mask = set_ends((jax.random.randint(keys[9], (FF,), 0, 4) < 3).astype(jnp.int32), jax.random.fold_in(keys[9], 1), 0, 1)
    return dict(cotangent=cotangent, inputs=inputs, gate_saved=gate_saved, up_saved=up_saved, gate_weight=gate_weight, up_weight=up_weight, down_weight=down_weight, scale_table=scale_table, scale_index=scale_index, clip_mask=clip_mask)


def walsh_signs(order_size):
    positions = jnp.arange(order_size, dtype=jnp.int32)
    common = jnp.bitwise_and(positions[:, None], positions[None, :])
    parity = jnp.zeros_like(common)
    shift_count = 0
    while 1 << shift_count < order_size:
        parity = parity + jnp.bitwise_and(jnp.right_shift(common, shift_count), 1)
        shift_count += 1
    return (1 - 2 * (parity % 2)).astype(jnp.float32)

def reference(cotangent, inputs, gate_saved, up_saved, gate_weight, up_weight, down_weight, scale_table, scale_index, clip_mask):
    down_grad = jnp.dot(cotangent, down_weight, preferred_element_type=jnp.float32)
    factor = scale_table[scale_index] * clip_mask.astype(jnp.float32)
    down_grad = down_grad * factor[None, :]
    blocks = down_grad.reshape(TOKENS, N_TENSOR, FF // (N_TENSOR * HB), HB)
    mixed = jnp.einsum('nsbc,ts,dc->ntbd', blocks, walsh_signs(N_TENSOR), walsh_signs(HB), precision=lax.Precision.HIGHEST)
    hidden_grad = mixed.reshape(TOKENS, FF) * (1.0 / math.sqrt(N_TENSOR * HB))
    gate = gate_saved.astype(jnp.float32)
    up_value = up_saved.astype(jnp.float32)
    sigmoid = jax.nn.sigmoid(gate)
    gate_grad = (hidden_grad * up_value * sigmoid * (1.0 + gate * (1.0 - sigmoid))).astype(jnp.bfloat16)
    up_grad = (hidden_grad * gate * sigmoid).astype(jnp.bfloat16)
    summed = jnp.dot(gate_grad, gate_weight.T, preferred_element_type=jnp.float32) + jnp.dot(up_grad, up_weight.T, preferred_element_type=jnp.float32)
    input_grad = summed.astype(jnp.bfloat16)
    rotation_grad = jnp.dot(inputs.T, input_grad, preferred_element_type=jnp.float32) * (1.0 / math.sqrt(TOKENS))
    return (input_grad, rotation_grad)
```

```python
import math

import jax
import jax.numpy as jnp
from jax import lax
from jax.sharding import PartitionSpec as P

HB = 128


def from_partner(shard, axis, apart):
    return lax.ppermute(shard, axis, [(i, i ^ 1 << apart) for i in range(lax.axis_size(axis))])


def walsh_signs(order_size):
    positions = jnp.arange(order_size, dtype=jnp.int32)
    common = jnp.bitwise_and(positions[:, None], positions[None, :])
    parity = jnp.zeros_like(common)
    shift_count = 0
    while 1 << shift_count < order_size:
        parity = parity + jnp.bitwise_and(jnp.right_shift(common, shift_count), 1)
        shift_count += 1
    return (1 - 2 * (parity % 2)).astype(jnp.float32)


def to_owners(summed, my_group, group_count, tensor_count):
    ratio = group_count // tensor_count
    blocks = summed.reshape(ratio, summed.shape[0] // ratio, summed.shape[1])
    position = my_group % ratio
    arrived = []
    for turn in range(ratio):
        pairs = []
        for i in range(group_count):
            for t in range(tensor_count):
                target = (ratio * t + (turn - i) % ratio) * tensor_count + i // ratio
                pairs.append((i * tensor_count + t, target))
        block = lax.dynamic_index_in_dim(blocks, (turn - position) % ratio, 0, keepdims=False)
        arrived.append(lax.ppermute(block, ("dp", "tensor"), pairs))
    order = jnp.stack(arrived)
    columns = [
        lax.dynamic_index_in_dim(order, (c + position) % ratio, 0, keepdims=False) for c in range(ratio)
    ]
    return jnp.concatenate(columns, axis=1)


def on_device(
    cotangent,
    inputs,
    gate_saved,
    up_saved,
    gate_weight,
    up_weight,
    down_weight,
    scale_table,
    scale_index,
    clip_mask,
):
    tok_rows, width = cotangent.shape
    hidden_dev = down_weight.shape[1]
    tensor_count = lax.axis_size("tensor")
    group_count = lax.axis_size("dp")
    my_group = lax.axis_index("dp")
    my_index = lax.axis_index("tensor")
    feature_rows = width // group_count
    share = tok_rows // tensor_count

    both = jnp.stack([cotangent, inputs])
    mine = lax.dynamic_slice_in_dim(both, my_index * share, share, axis=1)
    turned = lax.all_to_all(
        mine.reshape(2, share, group_count, feature_rows), "dp", split_axis=2, concat_axis=0, tiled=False
    )

    def whole(part):
        gathered = lax.all_gather(part, "tensor", axis=1)
        return gathered.reshape(group_count * tok_rows, feature_rows)

    cot_cols = whole(turned[:, 0])
    in_cols = whole(turned[:, 1])

    down_grad = lax.psum_scatter(
        jnp.dot(cot_cols, down_weight, preferred_element_type=jnp.float32).astype(jnp.bfloat16),
        "dp",
        scatter_dimension=0,
        tiled=True,
    ).astype(jnp.float32)
    levels = scale_table.shape[0]
    one_hot = (scale_index[:, None] == jnp.arange(levels, dtype=jnp.int32)[None, :]).astype(
        jnp.float32
    )
    factor = jnp.dot(one_hot, scale_table, precision=lax.Precision.HIGHEST) * clip_mask.astype(
        jnp.float32
    )
    down_grad = down_grad * factor[None, :]
    mixed = jnp.einsum(
        "nbc,dc->nbd",
        down_grad.reshape(tok_rows, hidden_dev // HB, HB),
        walsh_signs(HB),
        precision=lax.Precision.HIGHEST,
    ).reshape(tok_rows, hidden_dev)
    for bit_number in range(tensor_count.bit_length() - 1):
        partner = from_partner(mixed.astype(jnp.bfloat16), "tensor", bit_number).astype(jnp.float32)
        upper = jnp.bitwise_and(jnp.right_shift(my_index, bit_number), 1) == 1
        mixed = jnp.where(upper, partner - mixed, mixed + partner)
    hidden_grad = mixed * (1.0 / math.sqrt(tensor_count * HB))
    gate = gate_saved.astype(jnp.float32)
    up_value = up_saved.astype(jnp.float32)
    sigmoid = jax.nn.sigmoid(gate)
    gate_grad = (hidden_grad * up_value * sigmoid * (1.0 + gate * (1.0 - sigmoid))).astype(
        jnp.bfloat16
    )
    up_grad = (hidden_grad * gate * sigmoid).astype(jnp.bfloat16)
    pieces = lax.all_gather((gate_grad, up_grad), "dp", axis=0, tiled=True)
    first = lax.dot_general(
        pieces[0], gate_weight, (((1,), (1,)), ((), ())), preferred_element_type=jnp.float32
    )
    second = lax.dot_general(
        pieces[1], up_weight, (((1,), (1,)), ((), ())), preferred_element_type=jnp.float32
    )
    summed = lax.psum_scatter(first + second, "tensor", scatter_dimension=0, tiled=True).astype(
        jnp.bfloat16
    )
    input_grad = to_owners(summed, my_group, group_count, tensor_count)
    all_grad = lax.all_gather(input_grad, "dp", axis=0, tiled=True)
    rotation_grad = lax.dot_general(
        in_cols, all_grad, (((0,), (0,)), ((), ())), preferred_element_type=jnp.float32
    )
    rotation_grad = rotation_grad * (1.0 / math.sqrt(tok_rows * group_count))
    return (input_grad, rotation_grad)


def solution(mesh):
    placed = (
        P("dp", None),
        P("dp", None),
        P("dp", "tensor"),
        P("dp", "tensor"),
        P("dp", "tensor"),
        P("dp", "tensor"),
        P("dp", "tensor"),
        P(),
        P("tensor"),
        P("tensor"),
    )
    return jax.shard_map(
        on_device,
        mesh=mesh,
        in_specs=placed,
        out_specs=(P("dp", "tensor"), P("dp", "tensor")),
        check_vma=False,
    )
```

```python
import math

import jax
import jax.numpy as jnp
from jax import lax
from jax.experimental import pallas as pl
from jax.experimental.pallas import tpu as pltpu
from jax.sharding import PartitionSpec as P

HB = 128


def from_partner(shard, axis, apart):
    return lax.ppermute(shard, axis, [(i, i ^ 1 << apart) for i in range(lax.axis_size(axis))])


def walsh_signs(order_size):
    positions = jnp.arange(order_size, dtype=jnp.int32)
    common = jnp.bitwise_and(positions[:, None], positions[None, :])
    parity = jnp.zeros_like(common)
    shift_count = 0
    while 1 << shift_count < order_size:
        parity = parity + jnp.bitwise_and(jnp.right_shift(common, shift_count), 1)
        shift_count += 1
    return (1 - 2 * (parity % 2)).astype(jnp.float32)


LINE = 4
PAIR = 2


def spread(x_ref, gathered, send_sem, recv_sem, arrived):
    chunks = x_ref.shape[0]
    me = lax.axis_index("dp")
    z = lax.div(me, PAIR)
    y = lax.rem(me, PAIR)
    has_up = z < LINE - 1
    has_down = z > 0
    partner = z * PAIR + 1 - y
    targets = (me + PAIR, me - PAIR, partner)

    barrier = pltpu.get_barrier_semaphore()

    def greet(target):
        pl.semaphore_signal(
            barrier, inc=1, device_id={"dp": target}, device_id_type=pl.DeviceIdType.MESH
        )

    greet(partner)
    pl.when(has_up)(lambda: greet(targets[0]))
    pl.when(has_down)(lambda: greet(targets[1]))
    pl.semaphore_wait(barrier, 1 + has_up.astype(jnp.int32) + has_down.astype(jnp.int32))

    def copy(way, origin, slot, chunk, source):
        return pltpu.make_async_remote_copy(
            src_ref=source,
            dst_ref=gathered.at[slot, chunk],
            send_sem=send_sem.at[way, origin, chunk],
            recv_sem=recv_sem.at[slot, chunk],
            device_id={"dp": targets[way]},
            device_id_type=pl.DeviceIdType.MESH,
        )

    def held(slot, chunk):
        return gathered.at[slot, chunk]

    for chunk in range(chunks):
        pl.when(has_up)(lambda: copy(0, z, me, chunk, x_ref.at[chunk]).start())
        pl.when(has_down)(lambda: copy(1, z, me, chunk, x_ref.at[chunk]).start())
        copy(2, z, me, chunk, x_ref.at[chunk]).start()
    arrived(me, True)

    def take(slot, chunk):
        copy(2, z, slot, chunk, held(slot, chunk)).wait_recv()

    for apart in range(1, LINE):
        for chunk in range(chunks):
            for way, origin, goes_on in ((0, z - apart, has_up), (1, z + apart, has_down)):
                slot = origin * PAIR + y

                @pl.when((origin >= 0) & (origin < LINE))
                def _(way=way, origin=origin, goes_on=goes_on, slot=slot, chunk=chunk):
                    take(slot, chunk)
                    pl.when(goes_on)(lambda: copy(way, origin, slot, chunk, held(slot, chunk)).start())
                    copy(2, origin, slot, chunk, held(slot, chunk)).start()

        for origin in (z - apart, z + apart):
            pl.when((origin >= 0) & (origin < LINE))(
                lambda origin=origin: arrived(origin * PAIR + y, False)
            )
        if apart == 2:
            for chunk in range(chunks):
                take(partner, chunk)
            arrived(partner, False)

    for apart in range(1, LINE):
        for origin in (z - apart, z + apart):
            slot = origin * PAIR + 1 - y

            @pl.when((origin >= 0) & (origin < LINE))
            def _(slot=slot):
                for chunk in range(chunks):
                    take(slot, chunk)
                arrived(slot, False)

    for chunk in range(chunks):
        for origin in range(LINE):
            pl.when(has_up & (origin <= z))(
                lambda: copy(0, origin, me, chunk, x_ref.at[chunk]).wait_send()
            )
            pl.when(has_down & (origin >= z))(
                lambda: copy(1, origin, me, chunk, x_ref.at[chunk]).wait_send()
            )
            copy(2, origin, me, chunk, x_ref.at[chunk]).wait_send()


def gather_dot_kernel(
    x_ref, gate_hbm, up_hbm, out_ref, gathered, weights, weight_sem, send_sem, recv_sem
):
    rows = x_ref.shape[1]
    tile = 256
    loads = [
        pltpu.make_async_copy(source, weights.at[k], weight_sem.at[k])
        for k, source in enumerate((gate_hbm, up_hbm))
    ]
    for load in loads:
        load.start()

    def arrived(slot, own):
        if own:
            for load in loads:
                load.wait()
        to = pl.ds(pl.multiple_of(slot * rows, rows), rows)
        source = x_ref if own else gathered.at[slot]

        def step(n, carry):
            part = pl.ds(pl.multiple_of(n * tile, tile), tile)
            total = None
            for k in range(2):
                product = lax.dot_general(
                    source[k],
                    weights[k, part, :],
                    (((1,), (1,)), ((), ())),
                    preferred_element_type=jnp.float32,
                )
                total = product if total is None else total + product
            out_ref[to, part] = total
            return carry

        lax.fori_loop(0, weights.shape[1] // tile, step, 0)

    spread(x_ref, gathered, send_sem, recv_sem, arrived)


def gather_dot(grads, gate_weight, up_weight):
    chunks, rows, depth = grads.shape
    groups = LINE * PAIR
    features = gate_weight.shape[0]
    return pl.pallas_call(
        gather_dot_kernel,
        out_shape=jax.ShapeDtypeStruct((groups * rows, features), jnp.float32),
        in_specs=[
            pl.BlockSpec(memory_space=pltpu.VMEM),
            pl.BlockSpec(memory_space=pl.ANY),
            pl.BlockSpec(memory_space=pl.ANY),
        ],
        out_specs=pl.BlockSpec(memory_space=pltpu.VMEM),
        scratch_shapes=[
            pltpu.VMEM((groups, chunks, rows, depth), grads.dtype),
            pltpu.VMEM((2, features, depth), grads.dtype),
            pltpu.SemaphoreType.DMA((2,)),
            pltpu.SemaphoreType.DMA((3, LINE, chunks)),
            pltpu.SemaphoreType.DMA((groups, chunks)),
        ],
        compiler_params=pltpu.CompilerParams(
            collective_id=0, has_side_effects=True, vmem_limit_bytes=52 * 2**20
        ),
        cost_estimate=pl.CostEstimate(
            flops=4 * groups * rows * depth * features,
            bytes_accessed=4 * features * depth,
            transcendentals=0,
        ),
    )(grads, gate_weight, up_weight)


def gather_kernel(x_ref, out_ref, own_sem, send_sem, recv_sem):
    own_copy = pltpu.make_async_copy(x_ref, out_ref.at[lax.axis_index("dp")], own_sem)
    own_copy.start()
    spread(x_ref, out_ref, send_sem, recv_sem, lambda slot, own: None)
    own_copy.wait()


def gather_rows(shard):
    chunks = 4
    rows, columns = shard.shape
    groups = LINE * PAIR
    gathered = pl.pallas_call(
        gather_kernel,
        out_shape=jax.ShapeDtypeStruct((groups, chunks, rows // chunks, columns), shard.dtype),
        in_specs=[pl.BlockSpec(memory_space=pl.ANY)],
        out_specs=pl.BlockSpec(memory_space=pl.ANY),
        scratch_shapes=[
            pltpu.SemaphoreType.DMA,
            pltpu.SemaphoreType.DMA((3, LINE, chunks)),
            pltpu.SemaphoreType.DMA((groups, chunks)),
        ],
        compiler_params=pltpu.CompilerParams(collective_id=1, has_side_effects=True),
        cost_estimate=pl.CostEstimate(
            flops=0, bytes_accessed=groups * rows * columns * 2, transcendentals=0
        ),
    )(shard.reshape(chunks, rows // chunks, columns))
    return gathered.reshape(groups * rows, columns)


def sum_over_tensor(partial, my_index):
    count = lax.axis_size("tensor")
    current = partial.reshape(count, partial.shape[0] // count, partial.shape[1])
    for bit_number in range(count.bit_length() - 1):
        pairs = current.reshape(current.shape[0] // 2, 2, *current.shape[1:])
        mine = jnp.bitwise_and(jnp.right_shift(my_index, bit_number), 1)
        away = lax.dynamic_index_in_dim(pairs, 1 - mine, 1, keepdims=False).astype(jnp.bfloat16)
        kept = lax.dynamic_index_in_dim(pairs, mine, 1, keepdims=False)
        current = kept + from_partner(away, "tensor", bit_number).astype(jnp.float32)
    return current[0]


def to_owners(summed, my_group, group_count, tensor_count):
    ratio = group_count // tensor_count
    blocks = summed.reshape(ratio, summed.shape[0] // ratio, summed.shape[1])
    position = my_group % ratio
    arrived = []
    for turn in range(ratio):
        pairs = []
        for i in range(group_count):
            for t in range(tensor_count):
                target = (ratio * t + (turn - i) % ratio) * tensor_count + i // ratio
                pairs.append((i * tensor_count + t, target))
        block = lax.dynamic_index_in_dim(blocks, (turn - position) % ratio, 0, keepdims=False)
        arrived.append(lax.ppermute(block, ("dp", "tensor"), pairs))
    order = jnp.stack(arrived)
    columns = [
        lax.dynamic_index_in_dim(order, (c + position) % ratio, 0, keepdims=False) for c in range(ratio)
    ]
    return jnp.concatenate(columns, axis=1)


def on_device(
    cotangent,
    inputs,
    gate_saved,
    up_saved,
    gate_weight,
    up_weight,
    down_weight,
    scale_table,
    scale_index,
    clip_mask,
):
    tok_rows, width = cotangent.shape
    hidden_dev = down_weight.shape[1]
    tensor_count = lax.axis_size("tensor")
    group_count = lax.axis_size("dp")
    my_group = lax.axis_index("dp")
    my_index = lax.axis_index("tensor")
    feature_rows = width // group_count
    share = tok_rows // tensor_count

    both = jnp.stack([cotangent, inputs])
    mine = lax.dynamic_slice_in_dim(both, my_index * share, share, axis=1)
    turned = lax.all_to_all(
        mine.reshape(2, share, group_count, feature_rows), "dp", split_axis=2, concat_axis=0, tiled=False
    )

    def whole(part):
        gathered = lax.all_gather(part, "tensor", axis=1)
        return gathered.reshape(group_count * tok_rows, feature_rows)

    cot_cols = whole(turned[:, 0])
    in_cols = jnp.zeros((group_count, tensor_count, share, feature_rows), inputs.dtype)
    for turn in range(tensor_count):
        part = turned[:, 1]
        if turn:
            part = lax.ppermute(part, "tensor", [(i, i ^ turn) for i in range(tensor_count)])
        in_cols = lax.dynamic_update_index_in_dim(in_cols, part, my_index ^ turn, 1)
    in_cols = in_cols.reshape(group_count * tok_rows, feature_rows)

    down_grad = lax.psum_scatter(
        jnp.dot(cot_cols, down_weight, preferred_element_type=jnp.float32).astype(jnp.bfloat16),
        "dp",
        scatter_dimension=0,
        tiled=True,
    ).astype(jnp.float32)
    levels = scale_table.shape[0]
    one_hot = (scale_index[:, None] == jnp.arange(levels, dtype=jnp.int32)[None, :]).astype(
        jnp.float32
    )
    factor = jnp.dot(one_hot, scale_table, precision=lax.Precision.HIGHEST) * clip_mask.astype(
        jnp.float32
    )
    down_grad = down_grad * factor[None, :]
    mixed = jnp.einsum(
        "nbc,dc->nbd",
        down_grad.reshape(tok_rows, hidden_dev // HB, HB),
        walsh_signs(HB),
        precision=lax.Precision.HIGHEST,
    ).reshape(tok_rows, hidden_dev)
    for bit_number in range(tensor_count.bit_length() - 1):
        partner = from_partner(mixed.astype(jnp.bfloat16), "tensor", bit_number).astype(jnp.float32)
        upper = jnp.bitwise_and(jnp.right_shift(my_index, bit_number), 1) == 1
        mixed = jnp.where(upper, partner - mixed, mixed + partner)
    hidden_grad = mixed * (1.0 / math.sqrt(tensor_count * HB))
    gate = gate_saved.astype(jnp.float32)
    up_value = up_saved.astype(jnp.float32)
    sigmoid = jax.nn.sigmoid(gate)
    gate_grad = (hidden_grad * up_value * sigmoid * (1.0 + gate * (1.0 - sigmoid))).astype(
        jnp.bfloat16
    )
    up_grad = (hidden_grad * gate * sigmoid).astype(jnp.bfloat16)
    if group_count == LINE * PAIR:
        partial = gather_dot(jnp.stack([gate_grad, up_grad]), gate_weight, up_weight)
    else:
        pieces = lax.all_gather((gate_grad, up_grad), "dp", axis=0, tiled=True)
        partial = sum(
            lax.dot_general(piece, weight, (((1,), (1,)), ((), ())), preferred_element_type=jnp.float32)
            for piece, weight in zip(pieces, (gate_weight, up_weight))
        )
    summed = sum_over_tensor(partial, my_index).astype(jnp.bfloat16)
    input_grad = to_owners(summed, my_group, group_count, tensor_count)
    if group_count == LINE * PAIR:
        all_grad = gather_rows(input_grad)
    else:
        all_grad = lax.all_gather(input_grad, "dp", axis=0, tiled=True)
    rotation_grad = lax.dot_general(
        in_cols, all_grad, (((0,), (0,)), ((), ())), preferred_element_type=jnp.float32
    )
    rotation_grad = rotation_grad * (1.0 / math.sqrt(tok_rows * group_count))
    return (input_grad, rotation_grad)


def solution(mesh):
    placed = (
        P("dp", None),
        P("dp", None),
        P("dp", "tensor"),
        P("dp", "tensor"),
        P("dp", "tensor"),
        P("dp", "tensor"),
        P("dp", "tensor"),
        P(),
        P("tensor"),
        P("tensor"),
    )
    return jax.shard_map(
        on_device,
        mesh=mesh,
        in_specs=placed,
        out_specs=(P("dp", "tensor"), P("dp", "tensor")),
        check_vma=False,
    )
```

```python
import math

import jax
import jax.numpy as jnp
from jax import lax
from jax.experimental import pallas as pl
from jax.experimental.pallas import tpu as pltpu
from jax.sharding import PartitionSpec as P

HB = 128


def from_partner(shard, axis, apart):
    return lax.ppermute(shard, axis, [(i, i ^ 1 << apart) for i in range(lax.axis_size(axis))])


def walsh_signs(order_size):
    positions = jnp.arange(order_size, dtype=jnp.int32)
    common = jnp.bitwise_and(positions[:, None], positions[None, :])
    parity = jnp.zeros_like(common)
    shift_count = 0
    while 1 << shift_count < order_size:
        parity = parity + jnp.bitwise_and(jnp.right_shift(common, shift_count), 1)
        shift_count += 1
    return (1 - 2 * (parity % 2)).astype(jnp.float32)


LINE = 4
PAIR = 2


def spread(x_ref, gathered, send_sem, recv_sem, arrived):
    chunks = x_ref.shape[0]
    me = lax.axis_index("dp")
    z = lax.div(me, PAIR)
    y = lax.rem(me, PAIR)
    has_up = z < LINE - 1
    has_down = z > 0
    partner = z * PAIR + 1 - y
    targets = (me + PAIR, me - PAIR, partner)

    barrier = pltpu.get_barrier_semaphore()

    def greet(target):
        pl.semaphore_signal(
            barrier, inc=1, device_id={"dp": target}, device_id_type=pl.DeviceIdType.MESH
        )

    greet(partner)
    pl.when(has_up)(lambda: greet(targets[0]))
    pl.when(has_down)(lambda: greet(targets[1]))
    pl.semaphore_wait(barrier, 1 + has_up.astype(jnp.int32) + has_down.astype(jnp.int32))

    def copy(way, origin, slot, chunk, source):
        return pltpu.make_async_remote_copy(
            src_ref=source,
            dst_ref=gathered.at[slot, chunk],
            send_sem=send_sem.at[way, origin, chunk],
            recv_sem=recv_sem.at[slot, chunk],
            device_id={"dp": targets[way]},
            device_id_type=pl.DeviceIdType.MESH,
        )

    def held(slot, chunk):
        return gathered.at[slot, chunk]

    for chunk in range(chunks):
        pl.when(has_up)(lambda: copy(0, z, me, chunk, x_ref.at[chunk]).start())
        pl.when(has_down)(lambda: copy(1, z, me, chunk, x_ref.at[chunk]).start())
        copy(2, z, me, chunk, x_ref.at[chunk]).start()
    arrived(me, True)

    def take(slot, chunk):
        copy(2, z, slot, chunk, held(slot, chunk)).wait_recv()

    for apart in range(1, LINE):
        for chunk in range(chunks):
            for way, origin, goes_on in ((0, z - apart, has_up), (1, z + apart, has_down)):
                slot = origin * PAIR + y

                @pl.when((origin >= 0) & (origin < LINE))
                def _(way=way, origin=origin, goes_on=goes_on, slot=slot, chunk=chunk):
                    take(slot, chunk)
                    pl.when(goes_on)(lambda: copy(way, origin, slot, chunk, held(slot, chunk)).start())
                    copy(2, origin, slot, chunk, held(slot, chunk)).start()

        for origin in (z - apart, z + apart):
            pl.when((origin >= 0) & (origin < LINE))(
                lambda origin=origin: arrived(origin * PAIR + y, False)
            )
        if apart == 2:
            for chunk in range(chunks):
                take(partner, chunk)
            arrived(partner, False)

    for apart in range(1, LINE):
        for origin in (z - apart, z + apart):
            slot = origin * PAIR + 1 - y

            @pl.when((origin >= 0) & (origin < LINE))
            def _(slot=slot):
                for chunk in range(chunks):
                    take(slot, chunk)
                arrived(slot, False)

    for chunk in range(chunks):
        for origin in range(LINE):
            pl.when(has_up & (origin <= z))(
                lambda: copy(0, origin, me, chunk, x_ref.at[chunk]).wait_send()
            )
            pl.when(has_down & (origin >= z))(
                lambda: copy(1, origin, me, chunk, x_ref.at[chunk]).wait_send()
            )
            copy(2, origin, me, chunk, x_ref.at[chunk]).wait_send()


def gather_dot_kernel(
    x_ref, gate_hbm, up_hbm, out_ref, gathered, weights, weight_sem, send_sem, recv_sem
):
    rows = x_ref.shape[1]
    tile = 256
    loads = [
        pltpu.make_async_copy(source, weights.at[k], weight_sem.at[k])
        for k, source in enumerate((gate_hbm, up_hbm))
    ]
    for load in loads:
        load.start()

    def arrived(slot, own):
        if own:
            for load in loads:
                load.wait()
        to = pl.ds(pl.multiple_of(slot * rows, rows), rows)
        source = x_ref if own else gathered.at[slot]

        def step(n, carry):
            part = pl.ds(pl.multiple_of(n * tile, tile), tile)
            total = None
            for k in range(2):
                product = lax.dot_general(
                    source[k],
                    weights[k, part, :],
                    (((1,), (1,)), ((), ())),
                    preferred_element_type=jnp.float32,
                )
                total = product if total is None else total + product
            out_ref[to, part] = total
            return carry

        lax.fori_loop(0, weights.shape[1] // tile, step, 0)

    spread(x_ref, gathered, send_sem, recv_sem, arrived)


def gather_dot(grads, gate_weight, up_weight):
    chunks, rows, depth = grads.shape
    groups = LINE * PAIR
    features = gate_weight.shape[0]
    return pl.pallas_call(
        gather_dot_kernel,
        out_shape=jax.ShapeDtypeStruct((groups * rows, features), jnp.float32),
        in_specs=[
            pl.BlockSpec(memory_space=pltpu.VMEM),
            pl.BlockSpec(memory_space=pl.ANY),
            pl.BlockSpec(memory_space=pl.ANY),
        ],
        out_specs=pl.BlockSpec(memory_space=pltpu.VMEM),
        scratch_shapes=[
            pltpu.VMEM((groups, chunks, rows, depth), grads.dtype),
            pltpu.VMEM((2, features, depth), grads.dtype),
            pltpu.SemaphoreType.DMA((2,)),
            pltpu.SemaphoreType.DMA((3, LINE, chunks)),
            pltpu.SemaphoreType.DMA((groups, chunks)),
        ],
        compiler_params=pltpu.CompilerParams(
            collective_id=0, has_side_effects=True, vmem_limit_bytes=52 * 2**20
        ),
        cost_estimate=pl.CostEstimate(
            flops=4 * groups * rows * depth * features,
            bytes_accessed=4 * features * depth,
            transcendentals=0,
        ),
    )(grads, gate_weight, up_weight)


def gather_kernel(x_ref, out_ref, own_sem, send_sem, recv_sem):
    own_copy = pltpu.make_async_copy(x_ref, out_ref.at[lax.axis_index("dp")], own_sem)
    own_copy.start()
    spread(x_ref, out_ref, send_sem, recv_sem, lambda slot, own: None)
    own_copy.wait()


def gather_rows(shard):
    chunks = 4
    rows, columns = shard.shape
    groups = LINE * PAIR
    gathered = pl.pallas_call(
        gather_kernel,
        out_shape=jax.ShapeDtypeStruct((groups, chunks, rows // chunks, columns), shard.dtype),
        in_specs=[pl.BlockSpec(memory_space=pl.ANY)],
        out_specs=pl.BlockSpec(memory_space=pl.ANY),
        scratch_shapes=[
            pltpu.SemaphoreType.DMA,
            pltpu.SemaphoreType.DMA((3, LINE, chunks)),
            pltpu.SemaphoreType.DMA((groups, chunks)),
        ],
        compiler_params=pltpu.CompilerParams(collective_id=1, has_side_effects=True),
        cost_estimate=pl.CostEstimate(
            flops=0, bytes_accessed=groups * rows * columns * 2, transcendentals=0
        ),
    )(shard.reshape(chunks, rows // chunks, columns))
    return gathered.reshape(groups * rows, columns)


def sum_over_tensor(partial, my_index):
    count = lax.axis_size("tensor")
    current = partial.reshape(count, partial.shape[0] // count, partial.shape[1])
    for bit_number in range(count.bit_length() - 1):
        pairs = current.reshape(current.shape[0] // 2, 2, *current.shape[1:])
        mine = jnp.bitwise_and(jnp.right_shift(my_index, bit_number), 1)
        away = lax.dynamic_index_in_dim(pairs, 1 - mine, 1, keepdims=False).astype(jnp.bfloat16)
        kept = lax.dynamic_index_in_dim(pairs, mine, 1, keepdims=False)
        current = kept + from_partner(away, "tensor", bit_number).astype(jnp.float32)
    return current[0]


def to_owners(summed, my_group, group_count, tensor_count):
    ratio = group_count // tensor_count
    blocks = summed.reshape(ratio, summed.shape[0] // ratio, summed.shape[1])
    position = my_group % ratio
    arrived = []
    for turn in range(ratio):
        pairs = []
        for i in range(group_count):
            for t in range(tensor_count):
                target = (ratio * t + (turn - i) % ratio) * tensor_count + i // ratio
                pairs.append((i * tensor_count + t, target))
        block = lax.dynamic_index_in_dim(blocks, (turn - position) % ratio, 0, keepdims=False)
        arrived.append(lax.ppermute(block, ("dp", "tensor"), pairs))
    order = jnp.stack(arrived)
    columns = [
        lax.dynamic_index_in_dim(order, (c + position) % ratio, 0, keepdims=False) for c in range(ratio)
    ]
    return jnp.concatenate(columns, axis=1)


def on_device(
    cotangent,
    inputs,
    gate_saved,
    up_saved,
    gate_weight,
    up_weight,
    down_weight,
    scale_table,
    scale_index,
    clip_mask,
):
    tok_rows, width = cotangent.shape
    hidden_dev = down_weight.shape[1]
    tensor_count = lax.axis_size("tensor")
    group_count = lax.axis_size("dp")
    my_group = lax.axis_index("dp")
    my_index = lax.axis_index("tensor")
    feature_rows = width // group_count
    share = tok_rows // tensor_count

    both = jnp.stack([cotangent, inputs])
    mine = lax.dynamic_slice_in_dim(both, my_index * share, share, axis=1)
    turned = lax.all_to_all(
        mine.reshape(2, share, group_count, feature_rows), "dp", split_axis=2, concat_axis=0, tiled=False
    )

    def whole(part):
        gathered = lax.all_gather(part, "tensor", axis=1)
        return gathered.reshape(group_count * tok_rows, feature_rows)

    cot_cols = whole(turned[:, 0])
    in_cols = jnp.zeros((group_count, tensor_count, share, feature_rows), inputs.dtype)
    for turn in range(tensor_count):
        part = turned[:, 1]
        if turn:
            part = lax.ppermute(part, "tensor", [(i, i ^ turn) for i in range(tensor_count)])
        in_cols = lax.dynamic_update_index_in_dim(in_cols, part, my_index ^ turn, 1)
    in_cols = in_cols.reshape(group_count * tok_rows, feature_rows)

    down_grad = lax.psum_scatter(
        jnp.dot(cot_cols, down_weight, preferred_element_type=jnp.float32).astype(jnp.bfloat16),
        "dp",
        scatter_dimension=0,
        tiled=True,
    ).astype(jnp.float32)
    down_grad, in_cols = lax.optimization_barrier((down_grad, in_cols))
    levels = scale_table.shape[0]
    one_hot = (scale_index[:, None] == jnp.arange(levels, dtype=jnp.int32)[None, :]).astype(
        jnp.float32
    )
    factor = jnp.dot(one_hot, scale_table, precision=lax.Precision.HIGHEST) * clip_mask.astype(
        jnp.float32
    )
    down_grad = down_grad * factor[None, :]
    mixed = jnp.einsum(
        "nbc,dc->nbd",
        down_grad.reshape(tok_rows, hidden_dev // HB, HB),
        walsh_signs(HB),
        precision=lax.Precision.HIGHEST,
    ).reshape(tok_rows, hidden_dev)
    for bit_number in range(tensor_count.bit_length() - 1):
        partner = from_partner(mixed.astype(jnp.bfloat16), "tensor", bit_number).astype(jnp.float32)
        upper = jnp.bitwise_and(jnp.right_shift(my_index, bit_number), 1) == 1
        mixed = jnp.where(upper, partner - mixed, mixed + partner)
    hidden_grad = mixed * (1.0 / math.sqrt(tensor_count * HB))
    gate = gate_saved.astype(jnp.float32)
    up_value = up_saved.astype(jnp.float32)
    sigmoid = jax.nn.sigmoid(gate)
    gate_grad = (hidden_grad * up_value * sigmoid * (1.0 + gate * (1.0 - sigmoid))).astype(
        jnp.bfloat16
    )
    up_grad = (hidden_grad * gate * sigmoid).astype(jnp.bfloat16)
    if group_count == LINE * PAIR:
        partial = gather_dot(jnp.stack([gate_grad, up_grad]), gate_weight, up_weight)
    else:
        pieces = lax.all_gather((gate_grad, up_grad), "dp", axis=0, tiled=True)
        partial = sum(
            lax.dot_general(piece, weight, (((1,), (1,)), ((), ())), preferred_element_type=jnp.float32)
            for piece, weight in zip(pieces, (gate_weight, up_weight))
        )
    summed = sum_over_tensor(partial, my_index).astype(jnp.bfloat16)
    input_grad = to_owners(summed, my_group, group_count, tensor_count)
    if group_count == LINE * PAIR:
        all_grad = gather_rows(input_grad)
    else:
        all_grad = lax.all_gather(input_grad, "dp", axis=0, tiled=True)
    rotation_grad = lax.dot_general(
        in_cols, all_grad, (((0,), (0,)), ((), ())), preferred_element_type=jnp.float32
    )
    rotation_grad = rotation_grad * (1.0 / math.sqrt(tok_rows * group_count))
    return (input_grad, rotation_grad)


def solution(mesh):
    placed = (
        P("dp", None),
        P("dp", None),
        P("dp", "tensor"),
        P("dp", "tensor"),
        P("dp", "tensor"),
        P("dp", "tensor"),
        P("dp", "tensor"),
        P(),
        P("tensor"),
        P("tensor"),
    )
    return jax.shard_map(
        on_device,
        mesh=mesh,
        in_specs=placed,
        out_specs=(P("dp", "tensor"), P("dp", "tensor")),
        check_vma=False,
    )
```
